512 devices in a mesh: grp: 16 (over y, x), dev: 32 (over z, core).
Axes of the slice: x: 4, y: 4, z: 16, core: 2. Of those that a mesh axis runs over, the one named last changes fastest.
Arguments:
- particles: float32 [2048, 5, 128], P(('grp', 'dev')), as said below
- entropy: float32 [2048, 128], P(('grp', 'dev')), may hold values from 0.5 to 2
- lists: int32 [2048, 64], P(('grp', 'dev')), may hold values from 0 to 2047, as said below
- counts: int32 [2048], P(('grp', 'dev')), may hold values from 16 to 64, as said below
Outputs:
- density: float32 [2048, 128], P(('grp', 'dev'))
- accel: float32 [2048, 3, 128], P(('grp', 'dev'))
The draws below stay inside these ranges and needn't reach their ends.
Inputs may be any that keep to these rules, and one draw needn't show every extreme that they name: lists[c, 0] = c; every id lies in the group of c or in one of the two groups next to it, counting groups of 128 cells around a loop. `counts`: each count is a multiple of 16. `particles`: coordinates in 0 to 1 within the group's slab, masses positive, smoothing lengths from 0.3 to 0.6.
All inputs are finite; a program needn't handle non-finite values.
Results may differ from the reference program's by a relative error of at most 0.0003.
Values sent between devices are 32-bit elements; how exact they have to be, the bound alone decides.
A program may use at most 64 MiB of HBM per device.

```python
import math
import jax
import jax.numpy as jnp
from jax import lax

P_SIZE = 128
NB = 64
CG = 128
CELLS = 2048
N_GRP = 16


def draw_particles(key, part):
    key_pos = jax.random.fold_in(key, 11)
    key_mass = jax.random.fold_in(key, 12)
    key_smooth = jax.random.fold_in(key, 13)
    coords = jax.random.uniform(key_pos, (CELLS, 3, P_SIZE), jnp.float32)
    mass_log = jax.random.uniform(key_mass, (CELLS, 1, P_SIZE), jnp.float32, jnp.log(0.0003), jnp.log(0.0015))
    smooth = jax.random.uniform(key_smooth, (CELLS, 1, P_SIZE), jnp.float32, 0.3, 0.6)
    return jnp.concatenate([coords, jnp.exp(mass_log), smooth], axis=1).astype(jnp.float32)


def draw_lists(key, part):
    key_side = jax.random.fold_in(key, 21)
    key_rest = jax.random.fold_in(key, 22)
    cell_ids = jnp.arange(CELLS, dtype=jnp.int32)
    group_of = cell_ids // CG
    pick = jax.random.randint(key_side, (CELLS, NB), 0, 10, dtype=jnp.int32)
    shift_by = jnp.where(pick == 0, -1, jnp.where(pick == 1, 1, 0)).astype(jnp.int32)
    target = (group_of[:, None] + shift_by + N_GRP) % N_GRP
    within = jax.random.randint(key_rest, (CELLS, NB), 0, CG, dtype=jnp.int32)
    chosen = target * CG + within
    return chosen.at[:, 0].set(cell_ids).astype(jnp.int32)


def draw_counts(key, part):
    key_len = jax.random.fold_in(key, 31)
    quarter = jax.random.randint(key_len, (CELLS,), 1, 5, dtype=jnp.int32)
    values = quarter * (NB // 4)
    return values.at[0].set(NB).astype(jnp.int32)


def shard_levels(key, dims, pieces, low, high):
    gain = 1.0
    for axis_at, parts in pieces:
        heights = jax.random.uniform(jax.random.fold_in(jax.random.fold_in(key, 6), axis_at), (parts,), jnp.float32, low / len(pieces), high / len(pieces))
        gain = gain * jnp.repeat(jnp.exp(heights), dims[axis_at] // parts).reshape((-1,) + (1,) * (len(dims) - 1 - axis_at))
    return gain


def setup_inputs(seed: int = 0) -> dict:
    key_list = jax.random.split(jax.random.key(seed), 5)
    particles = draw_particles(jax.random.fold_in(key_list[4], 71), 0)
    entropy = jnp.clip(jnp.exp(math.log(2.0) - 1.3862944 * jax.random.uniform(key_list[1], (CELLS, P_SIZE), jnp.float32) ** shard_levels(key_list[1], (CELLS, P_SIZE), ((0, 512),), -0.2, 0.2)), 0.5, 2.0)
    lists = draw_lists(jax.random.fold_in(key_list[4], 71), 0)
    counts = draw_counts(jax.random.fold_in(key_list[4], 71), 0)
    return dict(particles=particles, entropy=entropy, lists=lists, counts=counts)


norm_const = 21.0 / (16.0 * math.pi)

def pair_offsets(center, others, side):
    unit_first = jnp.array([1.0, 0.0, 0.0], dtype=jnp.float32)
    offset = center[None, :3, :, None] - others[:, :3, None, :]
    offset = offset - side[:, None, None, None] * unit_first[None, :, None, None]
    dist_sq = lax.optimization_barrier(jnp.sum(offset * offset, axis=1))
    return (offset, dist_sq)

def kernel_parts(dist_sq, smooth):
    ratio = jnp.sqrt(dist_sq) / smooth
    base_of = jnp.maximum(1.0 - 0.5 * ratio, 0.0)
    kernel = norm_const / smooth ** 3 * base_of ** 4 * (1.0 + 2.0 * ratio)
    slope = -5.0 * norm_const / smooth ** 5 * base_of ** 3
    return (kernel, slope)

def reference(particles, entropy, lists, counts):
    slot_ids = jnp.arange(NB, dtype=jnp.int32)

    def side_for(cell_id):
        ids = lists[cell_id]
        shift = (ids // CG - cell_id // CG + 1 + N_GRP) % N_GRP - 1
        return shift.astype(jnp.float32)

    def density_cell(cell_id):
        center = particles[cell_id]
        others = particles[lists[cell_id]]
        live = (slot_ids < counts[cell_id]).astype(jnp.float32)
        offset, dist_sq = pair_offsets(center, others, side_for(cell_id))
        kernel, slope = kernel_parts(dist_sq, center[4][None, :, None])
        return lax.optimization_barrier(jnp.sum(live[:, None, None] * others[:, 3][:, None, :] * kernel, axis=(0, 2)))
    cell_range = jnp.arange(CELLS, dtype=jnp.int32)
    density = lax.map(density_cell, cell_range)
    pressure = entropy * density ** (5.0 / 3.0)
    weight = pressure / (density * density)

    def force_cell(cell_id):
        center = particles[cell_id]
        others = particles[lists[cell_id]]
        live = (slot_ids < counts[cell_id]).astype(jnp.float32)
        offset, dist_sq = pair_offsets(center, others, side_for(cell_id))
        kernel_i, slope_i = kernel_parts(dist_sq, center[4][None, :, None])
        kernel_j, slope_j = kernel_parts(dist_sq, others[:, 4][:, None, :])
        factor = live[:, None, None] * others[:, 3][:, None, :] * (weight[cell_id][None, :, None] * slope_i + weight[lists[cell_id]][:, None, :] * slope_j)
        return -lax.optimization_barrier(jnp.sum(factor[:, None] * offset, axis=(0, 3)))
    accel = lax.map(force_cell, cell_range)
    return (density, accel)
```

```python
import math

import jax
import jax.numpy as jnp
from jax import lax
from jax.experimental import pallas as pl
from jax.experimental.pallas import tpu as pltpu
from jax.sharding import PartitionSpec as P

MESH = pl.DeviceIdType.MESH
GROUPS = 16
ROWS = 16
CORES = 2
OWN = 4
LANES = 128
SLOTS = 64
GROUP_CELLS = ROWS * CORES * OWN
GROUP_BITS = 7
BLOCKS = 3 * CORES * ROWS
CELLS = BLOCKS * OWN
FEAT = 16
NORM = 21.0 / (16.0 * math.pi)
TINY = 1e-12


def block_at(region, core, row):
    return (region * ROWS + row) * CORES + core


def high(values):
    return values.astype(jnp.bfloat16).astype(jnp.float32)


def kernel(
    lists, counts, part, entropy, dens_out, acc_out,
    ext, hext, wext, feat, mom, left, invh, dist, cube, first,
    zsend, zrecv, fsend, frecv,
):
    grp = lax.axis_index("grp")
    dev = lax.axis_index("dev")
    row = dev // CORES
    core = dev % CORES
    mate = row * CORES + (1 - core)
    above = lax.rem(grp + 1, GROUPS)
    below = lax.rem(grp + GROUPS - 1, GROUPS)
    mine = block_at(1, core, row)
    targets = ((above, dev, 0), (below, dev, 2), (above, mate, 0), (below, mate, 2), (grp, mate, 1))

    def column(step):
        return lax.rem(row + step, ROWS) * CORES + core

    barrier = pltpu.get_barrier_semaphore()
    far_first = (8, 7, 9, 6, 10, 5, 11, 4, 12, 3, 13, 2, 14, 1, 15)
    for step in far_first:
        pl.semaphore_signal(barrier, inc=1, device_id=(grp, column(step)), device_id_type=MESH)
    for group, member, _ in targets:
        pl.semaphore_signal(barrier, inc=1, device_id=(group, member), device_id_type=MESH)

    rows_mine = pl.multiple_of(mine * OWN * 4, 16)
    for cell in range(OWN):
        ext[pl.ds(rows_mine + 4 * cell, 4), :] = part[cell, 0:4, :]
        hext[mine, cell : cell + 1, :] = part[cell, 4:5, :]

    def ext_block(at, count=1):
        return ext.at[pl.ds(pl.multiple_of(at * OWN * 4, 16), count * OWN * 4)]

    def h_block(at, count=1):
        return hext.at[pl.ds(at, count)]

    def w_block(at, count=1):
        return wext.at[pl.ds(at, count)]

    def send_column(which, block):
        for step in far_first:
            pltpu.make_async_remote_copy(
                src_ref=block(mine),
                dst_ref=block(mine),
                send_sem=zsend.at[which],
                recv_sem=zrecv.at[which, row],
                device_id=(grp, column(step)),
                device_id_type=MESH,
            ).start()

    def forward(which, block, at_row):
        at = block_at(1, core, at_row)
        for number, (group, member, region) in enumerate(targets):
            pltpu.make_async_remote_copy(
                src_ref=block(at),
                dst_ref=block(block_at(region, core, at_row)),
                send_sem=fsend.at[which, number],
                recv_sem=frecv.at[which, region],
                device_id=(group, member),
                device_id_type=MESH,
            ).start()

    def wait_for(ref, sem):
        pltpu.make_async_copy(ref, ref, sem).wait()

    def forward_rest(which, block):
        def step(number, carry):
            half = (number + 1) // 2
            at_row = lax.rem(row + ROWS + lax.rem(number, 2) * 2 * half - half, ROWS)
            wait_for(block(block_at(1, core, at_row)), zrecv.at[which, at_row])
            forward(which, block, at_row)
            return carry

        lax.fori_loop(1, ROWS, step, 0)

    def arrived(which, block):
        wait_for(block(block_at(1, 0, 0), ROWS), frecv.at[which, 1])
        wait_for(block(block_at(0, 0, 0), 2 * ROWS), frecv.at[which, 0])
        wait_for(block(block_at(2, 0, 0), 2 * ROWS), frecv.at[which, 2])

    def all_sent(which, block):
        wait_for(block(0, ROWS - 1), zsend.at[which])
        for number in range(len(targets)):
            wait_for(block(0, ROWS), fsend.at[which, number])

    pl.semaphore_wait(barrier, len(far_first) + len(targets))
    send_column(0, ext_block)
    forward(0, ext_block, row)
    send_column(1, h_block)
    forward(1, h_block, row)

    zero_row = jnp.zeros((1, LANES), jnp.float32)
    one_row = jnp.ones((1, LANES), jnp.float32)
    for cell in range(OWN):
        coords = [part[cell, axis : axis + 1, :] - 0.5 for axis in range(3)]
        highs = [high(value) for value in coords]
        lows = [high(value - top) for value, top in zip(coords, highs)]
        square = zero_row
        for top, low in zip(highs, lows):
            square = square + (top + low) * (top + low)
        part_a = high(square)
        part_b = high(square - part_a)
        part_c = square - part_a - part_b
        minus_high = [-2.0 * value for value in highs]
        minus_low = [-2.0 * value for value in lows]
        stacked = jnp.concatenate(
            minus_high + minus_high + [one_row] * 3 + [part_a, part_b, part_c] + [zero_row] * 4
            + minus_low + minus_low + [zero_row] * 10,
            axis=0,
        )
        wide = jnp.concatenate([stacked, jnp.zeros((LANES - 2 * FEAT, LANES), jnp.float32)], axis=0)
        left[cell] = wide.T[:, : 2 * FEAT].astype(jnp.bfloat16)
        invh[cell] = jnp.broadcast_to(2.0 / part[cell, 4:5, :], (LANES, LANES)).T

    def slot_cell(cell, number):
        ident = lists[cell, number]
        region = (lax.shift_right_logical(ident, GROUP_BITS) - grp + (GROUPS + 1)) & (GROUPS - 1)
        at = region * GROUP_CELLS + (ident & (GROUP_CELLS - 1))
        live = jnp.minimum(jnp.maximum(counts[cell] - number, 0), 1)
        return CELLS + live * (at - CELLS)

    feat[pl.ds(CELLS * FEAT, FEAT), :] = jnp.zeros((FEAT, LANES), jnp.float32)
    mom[pl.ds(CELLS * 8, 8), :] = jnp.zeros((8, LANES), jnp.float32)
    wext[BLOCKS] = jnp.zeros((OWN, LANES), jnp.float32)
    ones = jnp.ones((8, LANES), jnp.float32)
    zeros = jnp.zeros((8, LANES), jnp.float32)

    forward_rest(0, ext_block)
    forward_rest(1, h_block)
    arrived(0, ext_block)

    def features(number, carry):
        region = number // ROWS
        middle = 0.5 - (region - 1).astype(jnp.float32)

        def plane(axis):
            return ext[pl.ds(number * 32 + axis, 8, stride=4), :]

        coords = [plane(0) - middle, plane(1) - 0.5, plane(2) - 0.5]
        mass = plane(3)
        highs = [high(value) for value in coords]
        lows = [high(value - top) for value, top in zip(coords, highs)]
        square = zeros
        for top, low in zip(highs, lows):
            square = square + (top + low) * (top + low)
        part_a = high(square)
        part_b = high(square - part_a)
        part_c = square - part_a - part_b
        planes = highs + lows + [part_a, part_b, part_c, ones, ones, ones, mass, zeros, zeros, zeros]
        for at, value in enumerate(planes):
            feat[pl.ds(number * 8 * FEAT + at, 8, stride=FEAT), :] = value
        moments = [mass] + [mass * value for value in coords]
        for at, value in enumerate(moments + moments):
            mom[pl.ds(number * 64 + at, 8, stride=8), :] = value
        return carry

    lax.fori_loop(0, CELLS // 8, features, 0)

    def feature_rows(at):
        return feat[pl.ds(at * FEAT, FEAT), :]

    def density_cell(cell, carry):
        lhs = left[cell]
        scale = invh[cell]

        def step(pair, total):
            ids = [slot_cell(cell, 2 * pair + which) for which in range(2)]
            rows = [feature_rows(at) for at in ids]
            rhs = jnp.concatenate(rows, axis=1).astype(jnp.bfloat16)
            rhs = jnp.concatenate([rhs, rhs], axis=0)
            square = jnp.dot(lhs, rhs, preferred_element_type=jnp.float32)
            for which in range(2):
                part_sq = jnp.maximum(square[:, which * LANES : (which + 1) * LANES], TINY)
                gap = part_sq * lax.rsqrt(part_sq)
                dist[cell * SLOTS + 2 * pair + which] = gap
                base = jnp.maximum(4.0 - gap * scale, 0.0)
                base_sq = base * base
                total = total + base_sq * base_sq * (5.0 - base) * rows[which][12:13, :]
            return total

        total = lax.fori_loop(0, SLOTS // 2, step, jnp.zeros((LANES, LANES), jnp.float32))
        summed = jnp.sum(total.T, axis=0, keepdims=True)
        smooth = part[cell, 4:5, :]
        density = summed * (NORM / 256.0) / (smooth * smooth * smooth)
        weight = entropy[pl.ds(cell, 1), :] * jnp.exp(jnp.log(density) * (-1.0 / 3.0))
        dens_out[pl.ds(cell, 1), :] = density
        wext[mine, pl.ds(cell, 1), :] = weight
        return carry

    lax.fori_loop(0, OWN, density_cell, 0)

    send_column(2, w_block)
    forward(2, w_block, row)

    arrived(1, h_block)

    def smoothing(number, carry):
        smooth = jnp.concatenate([hext[2 * number], hext[2 * number + 1]], axis=0)
        inverse = 1.0 / smooth
        square = inverse * inverse
        feat[pl.ds(number * 8 * FEAT + 13, 8, stride=FEAT), :] = 2.0 * inverse
        feat[pl.ds(number * 8 * FEAT + 14, 8, stride=FEAT), :] = square * square * inverse
        return carry

    lax.fori_loop(0, CELLS // 8, smoothing, 0)

    upper = lax.broadcasted_iota(jnp.int32, (8, 2 * LANES), 0) < 4

    def split(values):
        top = high(values)
        return jnp.where(upper, top, values - top).astype(jnp.bfloat16)

    def moment_rows(at):
        return mom[pl.ds(at * 8, 8), :]

    across = (((1,), (1,)), ((), ()))

    def first_cell(cell, carry):
        scale = invh[cell]

        def step(pair, total):
            ids = [slot_cell(cell, 2 * pair + which) for which in range(2)]
            moments = jnp.concatenate([moment_rows(at) for at in ids], axis=1)
            cubes = []
            for which in range(2):
                gap = dist[cell * SLOTS + 2 * pair + which]
                base = jnp.maximum(4.0 - gap * scale, 0.0)
                cubes.append((base * base * base).astype(jnp.bfloat16))
                other = jnp.maximum(4.0 - gap * feature_rows(ids[which])[13:14, :], 0.0)
                cube[cell * SLOTS + 2 * pair + which] = (other * other * other).astype(jnp.bfloat16)
            return total + lax.dot_general(
                split(moments), jnp.concatenate(cubes, axis=1), across, preferred_element_type=jnp.float32
            )

        first[cell] = lax.fori_loop(0, SLOTS // 2, step, jnp.zeros((8, LANES), jnp.float32))
        return carry

    lax.fori_loop(0, OWN, first_cell, 0)
    forward_rest(2, w_block)
    arrived(2, w_block)

    def force_cell(cell, carry):
        def step(pair, total):
            ids = [slot_cell(cell, 2 * pair + which) for which in range(2)]
            scaled = []
            for at in ids:
                factor = wext[lax.shift_right_logical(at, 2), pl.ds(at & 3, 1), :] * feature_rows(at)[14:15, :]
                scaled.append(moment_rows(at) * factor)
            cubes = [cube[cell * SLOTS + 2 * pair + which] for which in range(2)]
            return total + lax.dot_general(
                split(jnp.concatenate(scaled, axis=1)),
                jnp.concatenate(cubes, axis=1),
                across,
                preferred_element_type=jnp.float32,
            )

        second = lax.fori_loop(0, SLOTS // 2, step, jnp.zeros((8, LANES), jnp.float32))
        second = second[0:4] + second[4:8]
        ahead = first[cell]
        ahead = ahead[0:4] + ahead[4:8]
        inverse = 1.0 / part[cell, 4:5, :]
        square = inverse * inverse
        own = wext[mine, pl.ds(cell, 1), :] * (square * square * inverse)
        joint = (own * ahead + second) * (5.0 * NORM / 64.0)
        coords = part[cell, 0:3, :] - 0.5
        acc_out[cell] = coords * joint[0:1] - joint[1:4]
        return carry

    lax.fori_loop(0, OWN, force_cell, 0)
    all_sent(0, ext_block)
    all_sent(1, h_block)
    all_sent(2, w_block)


def on_device(particles, entropy, lists, counts):
    vmem = pl.BlockSpec(memory_space=pltpu.VMEM)
    smem = pl.BlockSpec(memory_space=pltpu.SMEM)
    f32, bf16 = jnp.float32, jnp.bfloat16
    return pl.pallas_call(
        kernel,
        out_shape=(
            jax.ShapeDtypeStruct((OWN, LANES), f32),
            jax.ShapeDtypeStruct((OWN, 3, LANES), f32),
        ),
        in_specs=[smem, smem, vmem, vmem],
        out_specs=(vmem, vmem),
        scratch_shapes=[
            pltpu.VMEM((CELLS * 4, LANES), f32),
            pltpu.VMEM((BLOCKS, OWN, LANES), f32),
            pltpu.VMEM((BLOCKS + 1, OWN, LANES), f32),
            pltpu.VMEM(((CELLS + 1) * FEAT, LANES), f32),
            pltpu.VMEM(((CELLS + 1) * 8, LANES), f32),
            pltpu.VMEM((OWN, LANES, 2 * FEAT), bf16),
            pltpu.VMEM((OWN, LANES, LANES), f32),
            pltpu.VMEM((OWN * SLOTS, LANES, LANES), f32),
            pltpu.VMEM((OWN * SLOTS, LANES, LANES), bf16),
            pltpu.VMEM((OWN, 8, LANES), f32),
            pltpu.SemaphoreType.DMA((3,)),
            pltpu.SemaphoreType.DMA((3, ROWS)),
            pltpu.SemaphoreType.DMA((3, 5)),
            pltpu.SemaphoreType.DMA((3, 3)),
        ],
        compiler_params=pltpu.CompilerParams(
            collective_id=0, has_side_effects=True, vmem_limit_bytes=48 * 1024 * 1024
        ),
        name="sph",
    )(lists, counts, particles, entropy)


def solution(mesh):
    return jax.shard_map(
        on_device,
        mesh=mesh,
        in_specs=(
            P(("grp", "dev"), None, None),
            P(("grp", "dev"), None),
            P(("grp", "dev"), None),
            P(("grp", "dev")),
        ),
        out_specs=(P(("grp", "dev"), None), P(("grp", "dev"), None, None)),
        check_vma=False,
    )
```

```python
import math

import jax
import jax.numpy as jnp
from jax import lax
from jax.experimental import pallas as pl
from jax.experimental.pallas import tpu as pltpu
from jax.sharding import PartitionSpec as P

MESH = pl.DeviceIdType.MESH
GROUPS = 16
ROWS = 16
CORES = 2
OWN = 4
LANES = 128
SLOTS = 64
GROUP_CELLS = ROWS * CORES * OWN
GROUP_BITS = 7
BLOCKS = 3 * CORES * ROWS
CELLS = BLOCKS * OWN
FEAT = 16
NORM = 21.0 / (16.0 * math.pi)
TINY = 1e-12
DENSITY_PAIRS = 8
FIRST_SLOTS = 16
FORCE_SLOTS = 32


def block_at(region, core, row):
    return (region * ROWS + row) * CORES + core


def high(values):
    return values.astype(jnp.bfloat16).astype(jnp.float32)


def kernel(
    lists, counts, part, entropy, dens_out, acc_out,
    ext, hext, wext, feat, mom, left, invh, dist, cube, first,
    zsend, zrecv, fsend, frecv,
):
    grp = lax.axis_index("grp")
    dev = lax.axis_index("dev")
    row = dev // CORES
    core = dev % CORES
    mate = row * CORES + (1 - core)
    above = lax.rem(grp + 1, GROUPS)
    below = lax.rem(grp + GROUPS - 1, GROUPS)
    mine = block_at(1, core, row)
    targets = ((above, dev, 0), (below, dev, 2), (above, mate, 0), (below, mate, 2), (grp, mate, 1))

    def column(step):
        return lax.rem(row + step, ROWS) * CORES + core

    barrier = pltpu.get_barrier_semaphore()
    far_first = (8, 7, 9, 6, 10, 5, 11, 4, 12, 3, 13, 2, 14, 1, 15)
    for step in far_first:
        pl.semaphore_signal(barrier, inc=1, device_id=(grp, column(step)), device_id_type=MESH)
    for group, member, _ in targets:
        pl.semaphore_signal(barrier, inc=1, device_id=(group, member), device_id_type=MESH)

    rows_mine = pl.multiple_of(mine * OWN * 4, 16)
    for cell in range(OWN):
        ext[pl.ds(rows_mine + 4 * cell, 4), :] = part[cell, 0:4, :]
        hext[mine, cell : cell + 1, :] = part[cell, 4:5, :]

    def ext_block(at, count=1):
        return ext.at[pl.ds(pl.multiple_of(at * OWN * 4, 16), count * OWN * 4)]

    def h_block(at, count=1):
        return hext.at[pl.ds(at, count)]

    def w_block(at, count=1):
        return wext.at[pl.ds(at, count)]

    def send_column(which, block):
        for step in far_first:
            pltpu.make_async_remote_copy(
                src_ref=block(mine),
                dst_ref=block(mine),
                send_sem=zsend.at[which],
                recv_sem=zrecv.at[which, row],
                device_id=(grp, column(step)),
                device_id_type=MESH,
            ).start()

    def forward(which, block, at_row):
        at = block_at(1, core, at_row)
        for number, (group, member, region) in enumerate(targets):
            pltpu.make_async_remote_copy(
                src_ref=block(at),
                dst_ref=block(block_at(region, core, at_row)),
                send_sem=fsend.at[which, number],
                recv_sem=frecv.at[which, region],
                device_id=(group, member),
                device_id_type=MESH,
            ).start()

    def wait_for(ref, sem):
        pltpu.make_async_copy(ref, ref, sem).wait()

    def forward_rest(which, block):
        def step(number, carry):
            half = (number + 1) // 2
            at_row = lax.rem(row + ROWS + lax.rem(number, 2) * 2 * half - half, ROWS)
            wait_for(block(block_at(1, core, at_row)), zrecv.at[which, at_row])
            forward(which, block, at_row)
            return carry

        lax.fori_loop(1, ROWS, step, 0)

    def arrived(which, block):
        wait_for(block(block_at(1, 0, 0), ROWS), frecv.at[which, 1])
        wait_for(block(block_at(0, 0, 0), 2 * ROWS), frecv.at[which, 0])
        wait_for(block(block_at(2, 0, 0), 2 * ROWS), frecv.at[which, 2])

    def all_sent(which, block):
        wait_for(block(0, ROWS - 1), zsend.at[which])
        for number in range(len(targets)):
            wait_for(block(0, ROWS), fsend.at[which, number])

    pl.semaphore_wait(barrier, len(far_first) + len(targets))
    send_column(0, ext_block)
    forward(0, ext_block, row)
    send_column(1, h_block)
    forward(1, h_block, row)

    zero_row = jnp.zeros((1, LANES), jnp.float32)
    one_row = jnp.ones((1, LANES), jnp.float32)
    for cell in range(OWN):
        coords = [part[cell, axis : axis + 1, :] - 0.5 for axis in range(3)]
        highs = [high(value) for value in coords]
        lows = [high(value - top) for value, top in zip(coords, highs)]
        square = zero_row
        for top, low in zip(highs, lows):
            square = square + (top + low) * (top + low)
        part_a = high(square)
        part_b = high(square - part_a)
        part_c = square - part_a - part_b
        minus_high = [-2.0 * value for value in highs]
        minus_low = [-2.0 * value for value in lows]
        stacked = jnp.concatenate(
            minus_high + minus_high + [one_row] * 3 + [part_a, part_b, part_c] + [zero_row] * 4
            + minus_low + minus_low + [zero_row] * 10,
            axis=0,
        )
        wide = jnp.concatenate([stacked, jnp.zeros((LANES - 2 * FEAT, LANES), jnp.float32)], axis=0)
        left[cell] = wide.T[:, : 2 * FEAT].astype(jnp.bfloat16)
        invh[cell] = jnp.broadcast_to(2.0 / part[cell, 4:5, :], (LANES, LANES)).T

    def slot_cell(cell, number):
        ident = lists[cell, number]
        region = (lax.shift_right_logical(ident, GROUP_BITS) - grp + (GROUPS + 1)) & (GROUPS - 1)
        at = region * GROUP_CELLS + (ident & (GROUP_CELLS - 1))
        live = jnp.minimum(jnp.maximum(counts[cell] - number, 0), 1)
        return CELLS + live * (at - CELLS)

    feat[pl.ds(CELLS * FEAT, FEAT), :] = jnp.zeros((FEAT, LANES), jnp.float32)
    mom[pl.ds(CELLS * 8, 8), :] = jnp.zeros((8, LANES), jnp.float32)
    wext[BLOCKS] = jnp.zeros((OWN, LANES), jnp.float32)
    ones = jnp.ones((8, LANES), jnp.float32)
    zeros = jnp.zeros((8, LANES), jnp.float32)

    forward_rest(0, ext_block)
    forward_rest(1, h_block)
    arrived(0, ext_block)

    def features(number, carry):
        region = number // ROWS
        middle = 0.5 - (region - 1).astype(jnp.float32)

        def plane(axis):
            return ext[pl.ds(number * 32 + axis, 8, stride=4), :]

        coords = [plane(0) - middle, plane(1) - 0.5, plane(2) - 0.5]
        mass = plane(3)
        highs = [high(value) for value in coords]
        lows = [high(value - top) for value, top in zip(coords, highs)]
        square = zeros
        for top, low in zip(highs, lows):
            square = square + (top + low) * (top + low)
        part_a = high(square)
        part_b = high(square - part_a)
        part_c = square - part_a - part_b
        planes = highs + lows + [part_a, part_b, part_c, ones, ones, ones, mass, zeros, zeros, zeros]
        for at, value in enumerate(planes):
            feat[pl.ds(number * 8 * FEAT + at, 8, stride=FEAT), :] = value
        moments = [mass] + [mass * value for value in coords]
        for at, value in enumerate(moments + moments):
            mom[pl.ds(number * 64 + at, 8, stride=8), :] = value
        return carry

    lax.fori_loop(0, CELLS // 8, features, 0)

    def feature_rows(at):
        return feat[pl.ds(at * FEAT, FEAT), :]

    def density_cell(cell, carry):
        lhs = left[cell]
        scale = invh[cell]

        def step(turn, total):
            for pair in range(DENSITY_PAIRS):
                slot = (turn * DENSITY_PAIRS + pair) * 2
                rows = [feature_rows(slot_cell(cell, slot + which)) for which in range(2)]
                rhs = jnp.concatenate(rows, axis=1).astype(jnp.bfloat16)
                rhs = jnp.concatenate([rhs, rhs], axis=0)
                square = jnp.dot(lhs, rhs, preferred_element_type=jnp.float32)
                for which in range(2):
                    part_sq = jnp.maximum(square[:, which * LANES : (which + 1) * LANES], TINY)
                    gap = part_sq * lax.rsqrt(part_sq)
                    dist[cell * SLOTS + slot + which] = gap
                    base = jnp.maximum(4.0 - gap * scale, 0.0)
                    base_sq = base * base
                    total = total + base_sq * base_sq * (5.0 - base) * rows[which][12:13, :]
            return total

        total = lax.fori_loop(0, SLOTS // (2 * DENSITY_PAIRS), step, jnp.zeros((LANES, LANES), jnp.float32))
        summed = jnp.sum(total.T, axis=0, keepdims=True)
        smooth = part[cell, 4:5, :]
        density = summed * (NORM / 256.0) / (smooth * smooth * smooth)
        weight = entropy[pl.ds(cell, 1), :] * jnp.exp(jnp.log(density) * (-1.0 / 3.0))
        dens_out[pl.ds(cell, 1), :] = density
        wext[mine, pl.ds(cell, 1), :] = weight
        return carry

    lax.fori_loop(0, OWN, density_cell, 0)

    send_column(2, w_block)
    forward(2, w_block, row)

    arrived(1, h_block)

    def smoothing(number, carry):
        smooth = jnp.concatenate([hext[2 * number], hext[2 * number + 1]], axis=0)
        inverse = 1.0 / smooth
        square = inverse * inverse
        feat[pl.ds(number * 8 * FEAT + 13, 8, stride=FEAT), :] = 2.0 * inverse
        feat[pl.ds(number * 8 * FEAT + 14, 8, stride=FEAT), :] = square * square * inverse
        return carry

    lax.fori_loop(0, CELLS // 8, smoothing, 0)

    upper = lax.broadcasted_iota(jnp.int32, (8, LANES), 0) < 4

    def split(values):
        top = high(values)
        return jnp.where(upper, top, values - top).astype(jnp.bfloat16)

    def moment_rows(at):
        return mom[pl.ds(at * 8, 8), :]

    across = (((1,), (1,)), ((), ()))

    def first_cell(cell, carry):
        scale = invh[cell]

        def step(turn, total):
            tops, cubes = [], []
            for each in range(FIRST_SLOTS):
                slot = turn * FIRST_SLOTS + each
                at = slot_cell(cell, slot)
                tops.append(split(moment_rows(at)))
                gap = dist[cell * SLOTS + slot]
                base = jnp.maximum(4.0 - gap * scale, 0.0)
                cubes.append((base * base * base).astype(jnp.bfloat16))
                other = jnp.maximum(4.0 - gap * feature_rows(at)[13:14, :], 0.0)
                cube[cell * SLOTS + slot] = (other * other * other).astype(jnp.bfloat16)
            return total + lax.dot_general(
                jnp.concatenate(tops, axis=1), jnp.concatenate(cubes, axis=1), across,
                preferred_element_type=jnp.float32,
            )

        first[cell] = lax.fori_loop(0, SLOTS // FIRST_SLOTS, step, jnp.zeros((8, LANES), jnp.float32))
        return carry

    lax.fori_loop(0, OWN, first_cell, 0)
    forward_rest(2, w_block)
    arrived(2, w_block)

    def force_cell(cell, carry):
        def step(turn, total):
            tops, cubes = [], []
            for each in range(FORCE_SLOTS):
                slot = turn * FORCE_SLOTS + each
                at = slot_cell(cell, slot)
                factor = wext[lax.shift_right_logical(at, 2), pl.ds(at & 3, 1), :] * feature_rows(at)[14:15, :]
                tops.append(split(moment_rows(at) * factor))
                cubes.append(cube[cell * SLOTS + slot])
            return total + lax.dot_general(
                jnp.concatenate(tops, axis=1), jnp.concatenate(cubes, axis=1), across,
                preferred_element_type=jnp.float32,
            )

        second = lax.fori_loop(0, SLOTS // FORCE_SLOTS, step, jnp.zeros((8, LANES), jnp.float32))
        second = second[0:4] + second[4:8]
        ahead = first[cell]
        ahead = ahead[0:4] + ahead[4:8]
        inverse = 1.0 / part[cell, 4:5, :]
        square = inverse * inverse
        own = wext[mine, pl.ds(cell, 1), :] * (square * square * inverse)
        joint = (own * ahead + second) * (5.0 * NORM / 64.0)
        coords = part[cell, 0:3, :] - 0.5
        acc_out[cell] = coords * joint[0:1] - joint[1:4]
        return carry

    lax.fori_loop(0, OWN, force_cell, 0)
    all_sent(0, ext_block)
    all_sent(1, h_block)
    all_sent(2, w_block)


def on_device(particles, entropy, lists, counts):
    vmem = pl.BlockSpec(memory_space=pltpu.VMEM)
    smem = pl.BlockSpec(memory_space=pltpu.SMEM)
    f32, bf16 = jnp.float32, jnp.bfloat16
    return pl.pallas_call(
        kernel,
        out_shape=(
            jax.ShapeDtypeStruct((OWN, LANES), f32),
            jax.ShapeDtypeStruct((OWN, 3, LANES), f32),
        ),
        in_specs=[smem, smem, vmem, vmem],
        out_specs=(vmem, vmem),
        scratch_shapes=[
            pltpu.VMEM((CELLS * 4, LANES), f32),
            pltpu.VMEM((BLOCKS, OWN, LANES), f32),
            pltpu.VMEM((BLOCKS + 1, OWN, LANES), f32),
            pltpu.VMEM(((CELLS + 1) * FEAT, LANES), f32),
            pltpu.VMEM(((CELLS + 1) * 8, LANES), f32),
            pltpu.VMEM((OWN, LANES, 2 * FEAT), bf16),
            pltpu.VMEM((OWN, LANES, LANES), f32),
            pltpu.VMEM((OWN * SLOTS, LANES, LANES), f32),
            pltpu.VMEM((OWN * SLOTS, LANES, LANES), bf16),
            pltpu.VMEM((OWN, 8, LANES), f32),
            pltpu.SemaphoreType.DMA((3,)),
            pltpu.SemaphoreType.DMA((3, ROWS)),
            pltpu.SemaphoreType.DMA((3, 5)),
            pltpu.SemaphoreType.DMA((3, 3)),
        ],
        compiler_params=pltpu.CompilerParams(
            collective_id=0, has_side_effects=True, vmem_limit_bytes=48 * 1024 * 1024
        ),
        name="sph",
    )(lists, counts, particles, entropy)


def solution(mesh):
    return jax.shard_map(
        on_device,
        mesh=mesh,
        in_specs=(
            P(("grp", "dev"), None, None),
            P(("grp", "dev"), None),
            P(("grp", "dev"), None),
            P(("grp", "dev")),
        ),
        out_specs=(P(("grp", "dev"), None), P(("grp", "dev"), None, None)),
        check_vma=False,
    )
```

```python
import math

import jax
import jax.numpy as jnp
from jax import lax
from jax.experimental import pallas as pl
from jax.experimental.pallas import tpu as pltpu
from jax.sharding import PartitionSpec as P

MESH = pl.DeviceIdType.MESH
GROUPS = 16
ROWS = 16
CORES = 2
OWN = 4
LANES = 128
SLOTS = 64
GROUP_CELLS = ROWS * CORES * OWN
GROUP_BITS = 7
BLOCKS = 3 * CORES * ROWS
CELLS = BLOCKS * OWN
FEAT = 16
NORM = 21.0 / (16.0 * math.pi)
TINY = 1e-12
DENSITY_PAIRS = 16
FIRST_SLOTS = 16
FORCE_SLOTS = 64


def block_at(region, core, row):
    return (region * CORES + core) * ROWS + row


def high(values):
    return values.astype(jnp.bfloat16).astype(jnp.float32)


def kernel(
    lists, counts, part, entropy, dens_out, acc_out,
    ext, hext, wext, feat, mom, left, invh, dist, cube, first,
    zsend, zrecv, fsend, frecv,
):
    grp = lax.axis_index("grp")
    dev = lax.axis_index("dev")
    row = dev // CORES
    core = dev % CORES
    mate = row * CORES + (1 - core)
    above = lax.rem(grp + 1, GROUPS)
    below = lax.rem(grp + GROUPS - 1, GROUPS)
    mine = block_at(1, core, row)
    targets = ((above, dev, 0), (below, dev, 2), (above, mate, 0), (below, mate, 2), (grp, mate, 1))

    def column(step):
        return lax.rem(row + step, ROWS) * CORES + core

    barrier = pltpu.get_barrier_semaphore()
    near = (1, 15, 2, 14, 3, 13, 4, 12)
    far = (8, 7, 9, 6, 10, 5, 11)
    for step in near:
        pl.semaphore_signal(barrier, inc=1, device_id=(grp, column(step)), device_id_type=MESH)
    for group, member, _ in targets:
        pl.semaphore_signal(barrier, inc=1, device_id=(group, member), device_id_type=MESH)

    rows_mine = pl.multiple_of(mine * OWN * 4, 16)
    for cell in range(OWN):
        ext[pl.ds(rows_mine + 4 * cell, 4), :] = part[cell, 0:4, :]
        hext[mine, cell : cell + 1, :] = part[cell, 4:5, :]

    def ext_block(at, count=1):
        return ext.at[pl.ds(pl.multiple_of(at * OWN * 4, 16), count * OWN * 4)]

    def h_block(at, count=1):
        return hext.at[pl.ds(at, count)]

    def w_block(at, count=1):
        return wext.at[pl.ds(at, count)]

    def send_row(which, block, at_row, step):
        at = block_at(1, core, at_row)
        pltpu.make_async_remote_copy(
            src_ref=block(at),
            dst_ref=block(at),
            send_sem=zsend.at[which],
            recv_sem=zrecv.at[which, at_row],
            device_id=(grp, column(step)),
            device_id_type=MESH,
        ).start()

    def forward(which, block, at_row, count):
        at = block_at(1, core, at_row)
        for number, (group, member, region) in enumerate(targets):
            pltpu.make_async_remote_copy(
                src_ref=block(at, count),
                dst_ref=block(block_at(region, core, at_row), count),
                send_sem=fsend.at[which, number],
                recv_sem=frecv.at[which, region],
                device_id=(group, member),
                device_id_type=MESH,
            ).start()

    def wait_for(ref, sem):
        pltpu.make_async_copy(ref, ref, sem).wait()

    def landed(which, block, at_row):
        wait_for(block(block_at(1, core, at_row)), zrecv.at[which, at_row])

    def row_at(number):
        half = (number + 1) // 2
        return lax.rem(row + ROWS + lax.rem(number, 2) * 2 * half - half, ROWS)

    def pass_on(which, block):
        forward(which, block, row, 1)

        def close(number, carry):
            at_row = row_at(number)
            landed(which, block, at_row)
            send_row(which, block, at_row, ROWS + 4 - 8 * lax.rem(number, 2))
            forward(which, block, at_row, 1)
            return carry

        def rest(number, carry):
            at_row = row_at(number)
            landed(which, block, at_row)
            forward(which, block, at_row, 1)
            return carry

        lax.fori_loop(1, 7, close, 0)
        rest(jnp.int32(7), 0)
        at_row = lax.rem(row + ROWS - 4, ROWS)
        landed(which, block, at_row)
        send_row(which, block, at_row, 4)
        forward(which, block, at_row, 1)
        lax.fori_loop(9, ROWS, rest, 0)

    def pass_whole(which, block):
        def one(number, carry):
            landed(which, block, lax.rem(row + number, ROWS))
            return carry

        lax.fori_loop(1, ROWS, one, 0)
        forward(which, block, 0, ROWS)

    def arrived(which, block):
        wait_for(block(block_at(1, 0, 0), ROWS), frecv.at[which, 1])
        wait_for(block(block_at(0, 0, 0), 2 * ROWS), frecv.at[which, 0])
        wait_for(block(block_at(2, 0, 0), 2 * ROWS), frecv.at[which, 2])

    def all_sent(which, block):
        wait_for(block(0, ROWS - 1), zsend.at[which])
        for number in range(len(targets)):
            wait_for(block(0, ROWS), fsend.at[which, number])

    pl.semaphore_wait(barrier, len(near) + len(targets))
    for step in near:
        send_row(0, ext_block, row, step)
    for step in near:
        send_row(1, h_block, row, step)

    zero_row = jnp.zeros((1, LANES), jnp.float32)
    one_row = jnp.ones((1, LANES), jnp.float32)
    for cell in range(OWN):
        coords = [part[cell, axis : axis + 1, :] - 0.5 for axis in range(3)]
        highs = [high(value) for value in coords]
        lows = [high(value - top) for value, top in zip(coords, highs)]
        square = zero_row
        for top, low in zip(highs, lows):
            square = square + (top + low) * (top + low)
        part_a = high(square)
        part_b = high(square - part_a)
        part_c = square - part_a - part_b
        minus_high = [-2.0 * value for value in highs]
        minus_low = [-2.0 * value for value in lows]
        stacked = jnp.concatenate(
            minus_high + minus_high + [one_row] * 3 + [part_a, part_b, part_c] + [zero_row] * 4
            + minus_low + minus_low + [zero_row] * 10,
            axis=0,
        )
        wide = jnp.concatenate([stacked, jnp.zeros((LANES - 2 * FEAT, LANES), jnp.float32)], axis=0)
        left[cell] = wide.T[:, : 2 * FEAT].astype(jnp.bfloat16)
        invh[cell] = jnp.broadcast_to(2.0 / part[cell, 4:5, :], (LANES, LANES)).T

    def slot_cell(cell, number):
        ident = lists[cell, number]
        region = (lax.shift_right_logical(ident, GROUP_BITS) - grp + (GROUPS + 1)) & (GROUPS - 1)
        plane = lax.shift_left(ident & OWN, 4)
        at = region * GROUP_CELLS + plane + (lax.shift_right_logical(ident, 1) & 60) + (ident & (OWN - 1))
        live = jnp.minimum(jnp.maximum(counts[cell] - number, 0), 1)
        return CELLS + live * (at - CELLS)

    feat[pl.ds(CELLS * FEAT, FEAT), :] = jnp.zeros((FEAT, LANES), jnp.float32)
    mom[pl.ds(CELLS * 8, 8), :] = jnp.zeros((8, LANES), jnp.float32)
    wext[BLOCKS] = jnp.zeros((OWN, LANES), jnp.float32)
    ones = jnp.ones((8, LANES), jnp.float32)
    zeros = jnp.zeros((8, LANES), jnp.float32)

    def settle(number, carry):
        rows = number * 8 * FEAT
        for at in (9, 10, 11):
            feat[pl.ds(rows + at, 8, stride=FEAT), :] = ones
        for at in (13, 14, 15):
            feat[pl.ds(rows + at, 8, stride=FEAT), :] = zeros
        return carry

    lax.fori_loop(0, CELLS // 8, settle, 0)
    pass_on(0, ext_block)
    for step in far:
        send_row(1, h_block, row, step)
    arrived(0, ext_block)

    def planes(number):
        region = number // ROWS
        middle = 0.5 - (region - 1).astype(jnp.float32)

        def plane(axis):
            return ext[pl.ds(number * 32 + axis, 8, stride=4), :]

        return [plane(0) - middle, plane(1) - 0.5, plane(2) - 0.5], plane(3)

    def features(number, carry):
        coords, mass = planes(number)
        highs = [high(value) for value in coords]
        lows = [high(value - top) for value, top in zip(coords, highs)]
        square = zeros
        for top, low in zip(highs, lows):
            square = square + (top + low) * (top + low)
        part_a = high(square)
        part_b = high(square - part_a)
        part_c = square - part_a - part_b
        for at, value in enumerate(highs + lows + [part_a, part_b, part_c]):
            feat[pl.ds(number * 8 * FEAT + at, 8, stride=FEAT), :] = value
        feat[pl.ds(number * 8 * FEAT + 12, 8, stride=FEAT), :] = mass
        return carry

    lax.fori_loop(0, CELLS // 8, features, 0)

    def feature_rows(at):
        return feat[pl.ds(at * FEAT, FEAT), :]

    def density_cell(cell, carry):
        lhs = left[cell]
        scale = invh[cell]

        def step(turn, total):
            for pair in range(DENSITY_PAIRS):
                slot = (turn * DENSITY_PAIRS + pair) * 2
                rows = [feature_rows(slot_cell(cell, slot + which)) for which in range(2)]
                rhs = jnp.concatenate(rows, axis=1).astype(jnp.bfloat16)
                rhs = jnp.concatenate([rhs, rhs], axis=0)
                square = jnp.dot(lhs, rhs, preferred_element_type=jnp.float32)
                for which in range(2):
                    part_sq = jnp.maximum(square[:, which * LANES : (which + 1) * LANES], TINY)
                    gap = part_sq * lax.rsqrt(part_sq)
                    dist[cell * SLOTS + slot + which] = gap
                    base = jnp.maximum(4.0 - gap * scale, 0.0)
                    base_sq = base * base
                    total = total + base_sq * base_sq * (5.0 - base) * rows[which][12:13, :]
            return total

        total = lax.fori_loop(0, SLOTS // (2 * DENSITY_PAIRS), step, jnp.zeros((LANES, LANES), jnp.float32))
        summed = jnp.sum(total.T, axis=0, keepdims=True)
        smooth = part[cell, 4:5, :]
        density = summed * (NORM / 256.0) / (smooth * smooth * smooth)
        weight = entropy[pl.ds(cell, 1), :] * jnp.exp(jnp.log(density) * (-1.0 / 3.0))
        dens_out[pl.ds(cell, 1), :] = density
        wext[mine, pl.ds(cell, 1), :] = weight
        return carry

    lax.fori_loop(0, OWN, density_cell, 0)

    for step in far + near:
        send_row(2, w_block, row, step)

    pass_whole(1, h_block)

    def moments(number, carry):
        coords, mass = planes(number)
        values = [mass] + [mass * value for value in coords]
        for at, value in enumerate(values + values):
            mom[pl.ds(number * 64 + at, 8, stride=8), :] = value
        return carry

    lax.fori_loop(0, CELLS // 8, moments, 0)

    def smoothing(number, carry):
        smooth = jnp.concatenate([hext[2 * number], hext[2 * number + 1]], axis=0)
        inverse = 1.0 / smooth
        square = inverse * inverse
        feat[pl.ds(number * 8 * FEAT + 13, 8, stride=FEAT), :] = 2.0 * inverse
        feat[pl.ds(number * 8 * FEAT + 14, 8, stride=FEAT), :] = square * square * inverse
        return carry


    upper = lax.broadcasted_iota(jnp.int32, (8, LANES), 0) < 4

    def split(values):
        top = high(values)
        return jnp.where(upper, top, values - top).astype(jnp.bfloat16)

    def moment_rows(at):
        return mom[pl.ds(at * 8, 8), :]

    across = (((1,), (1,)), ((), ()))

    def first_cell(cell, carry):
        scale = invh[cell]

        def step(turn, total):
            tops, cubes = [], []
            for each in range(FIRST_SLOTS):
                slot = turn * FIRST_SLOTS + each
                at = slot_cell(cell, slot)
                tops.append(split(moment_rows(at)))
                gap = dist[cell * SLOTS + slot]
                base = jnp.maximum(4.0 - gap * scale, 0.0)
                cubes.append((base * base * base).astype(jnp.bfloat16))
            return total + lax.dot_general(
                jnp.concatenate(tops, axis=1), jnp.concatenate(cubes, axis=1), across,
                preferred_element_type=jnp.float32,
            )

        first[cell] = lax.fori_loop(0, SLOTS // FIRST_SLOTS, step, jnp.zeros((8, LANES), jnp.float32))
        return carry

    lax.fori_loop(0, OWN, first_cell, 0)
    arrived(1, h_block)
    lax.fori_loop(0, CELLS // 8, smoothing, 0)

    def cube_cell(cell, carry):
        def step(turn, inner):
            for each in range(FIRST_SLOTS):
                slot = turn * FIRST_SLOTS + each
                scale = feature_rows(slot_cell(cell, slot))[13:14, :]
                other = jnp.maximum(4.0 - dist[cell * SLOTS + slot] * scale, 0.0)
                cube[cell * SLOTS + slot] = (other * other * other).astype(jnp.bfloat16)
            return inner

        return lax.fori_loop(0, SLOTS // FIRST_SLOTS, step, carry)

    lax.fori_loop(0, OWN - 2, cube_cell, 0)
    pass_whole(2, w_block)
    lax.fori_loop(OWN - 2, OWN, cube_cell, 0)
    arrived(2, w_block)

    def force_cell(cell, carry):
        def step(turn, total):
            tops, cubes = [], []
            for each in range(FORCE_SLOTS):
                slot = turn * FORCE_SLOTS + each
                at = slot_cell(cell, slot)
                factor = wext[lax.shift_right_logical(at, 2), pl.ds(at & 3, 1), :] * feature_rows(at)[14:15, :]
                tops.append(split(moment_rows(at) * factor))
                cubes.append(cube[cell * SLOTS + slot])
            return total + lax.dot_general(
                jnp.concatenate(tops, axis=1), jnp.concatenate(cubes, axis=1), across,
                preferred_element_type=jnp.float32,
            )

        second = lax.fori_loop(0, SLOTS // FORCE_SLOTS, step, jnp.zeros((8, LANES), jnp.float32))
        second = second[0:4] + second[4:8]
        ahead = first[cell]
        ahead = ahead[0:4] + ahead[4:8]
        inverse = 1.0 / part[cell, 4:5, :]
        square = inverse * inverse
        own = wext[mine, pl.ds(cell, 1), :] * (square * square * inverse)
        joint = (own * ahead + second) * (5.0 * NORM / 64.0)
        coords = part[cell, 0:3, :] - 0.5
        acc_out[cell] = coords * joint[0:1] - joint[1:4]
        return carry

    lax.fori_loop(0, OWN, force_cell, 0)
    all_sent(0, ext_block)
    all_sent(1, h_block)
    all_sent(2, w_block)


def on_device(particles, entropy, lists, counts):
    vmem = pl.BlockSpec(memory_space=pltpu.VMEM)
    smem = pl.BlockSpec(memory_space=pltpu.SMEM)
    f32, bf16 = jnp.float32, jnp.bfloat16
    return pl.pallas_call(
        kernel,
        out_shape=(
            jax.ShapeDtypeStruct((OWN, LANES), f32),
            jax.ShapeDtypeStruct((OWN, 3, LANES), f32),
        ),
        in_specs=[smem, smem, vmem, vmem],
        out_specs=(vmem, vmem),
        scratch_shapes=[
            pltpu.VMEM((CELLS * 4, LANES), f32),
            pltpu.VMEM((BLOCKS, OWN, LANES), f32),
            pltpu.VMEM((BLOCKS + 1, OWN, LANES), f32),
            pltpu.VMEM(((CELLS + 1) * FEAT, LANES), f32),
            pltpu.VMEM(((CELLS + 1) * 8, LANES), f32),
            pltpu.VMEM((OWN, LANES, 2 * FEAT), bf16),
            pltpu.VMEM((OWN, LANES, LANES), f32),
            pltpu.VMEM((OWN * SLOTS, LANES, LANES), f32),
            pltpu.VMEM((OWN * SLOTS, LANES, LANES), bf16),
            pltpu.VMEM((OWN, 8, LANES), f32),
            pltpu.SemaphoreType.DMA((3,)),
            pltpu.SemaphoreType.DMA((3, ROWS)),
            pltpu.SemaphoreType.DMA((3, 5)),
            pltpu.SemaphoreType.DMA((3, 3)),
        ],
        compiler_params=pltpu.CompilerParams(
            collective_id=0, has_side_effects=True, vmem_limit_bytes=48 * 1024 * 1024
        ),
        name="sph",
    )(lists, counts, particles, entropy)


def solution(mesh):
    return jax.shard_map(
        on_device,
        mesh=mesh,
        in_specs=(
            P(("grp", "dev"), None, None),
            P(("grp", "dev"), None),
            P(("grp", "dev"), None),
            P(("grp", "dev")),
        ),
        out_specs=(P(("grp", "dev"), None), P(("grp", "dev"), None, None)),
        check_vma=False,
    )
```

```python
import math

import jax
import jax.numpy as jnp
from jax import lax
from jax.experimental import pallas as pl
from jax.experimental.pallas import tpu as pltpu
from jax.sharding import PartitionSpec as P

MESH = pl.DeviceIdType.MESH
GROUPS = 16
ROWS = 16
CORES = 2
OWN = 4
LANES = 128
SLOTS = 64
GROUP_CELLS = ROWS * CORES * OWN
GROUP_BITS = 7
BLOCKS = 3 * CORES * ROWS
CELLS = BLOCKS * OWN
FEAT = 16
NORM = 21.0 / (16.0 * math.pi)
TINY = 1e-12
DENSITY_PAIRS = 32
FIRST_SLOTS = 16
FORCE_SLOTS = 64


def block_at(region, core, row):
    return (region * CORES + core) * ROWS + row


def high(values):
    return values.astype(jnp.bfloat16).astype(jnp.float32)


def kernel(
    lists, counts, part, entropy, dens_out, acc_out,
    ext, hext, wext, feat, mom, left, invh, dist, cube, first,
    zsend, zrecv, fsend, frecv,
):
    grp = lax.axis_index("grp")
    dev = lax.axis_index("dev")
    row = dev // CORES
    core = dev % CORES
    mate = row * CORES + (1 - core)
    above = lax.rem(grp + 1, GROUPS)
    below = lax.rem(grp + GROUPS - 1, GROUPS)
    mine = block_at(1, core, row)
    targets = ((above, dev, 0), (below, dev, 2), (above, mate, 0), (below, mate, 2), (grp, mate, 1))

    def column(step):
        return lax.rem(row + step, ROWS) * CORES + core

    barrier = pltpu.get_barrier_semaphore()
    near = (1, 15, 2, 14, 3, 13, 4, 12)
    far = (8, 7, 9, 6, 10, 5, 11)
    for step in near:
        pl.semaphore_signal(barrier, inc=1, device_id=(grp, column(step)), device_id_type=MESH)
    for group, member, _ in targets:
        pl.semaphore_signal(barrier, inc=1, device_id=(group, member), device_id_type=MESH)

    rows_mine = pl.multiple_of(mine * OWN * 4, 16)
    for cell in range(OWN):
        ext[pl.ds(rows_mine + 4 * cell, 4), :] = part[cell, 0:4, :]
        hext[mine, cell : cell + 1, :] = part[cell, 4:5, :]

    def ext_block(at, count=1):
        return ext.at[pl.ds(pl.multiple_of(at * OWN * 4, 16), count * OWN * 4)]

    def h_block(at, count=1):
        return hext.at[pl.ds(at, count)]

    def w_block(at, count=1):
        return wext.at[pl.ds(at, count)]

    def send_row(which, block, at_row, step):
        at = block_at(1, core, at_row)
        pltpu.make_async_remote_copy(
            src_ref=block(at),
            dst_ref=block(at),
            send_sem=zsend.at[which],
            recv_sem=zrecv.at[which, at_row],
            device_id=(grp, column(step)),
            device_id_type=MESH,
        ).start()

    def forward(which, block, at_row, count):
        at = block_at(1, core, at_row)
        for number, (group, member, region) in enumerate(targets):
            pltpu.make_async_remote_copy(
                src_ref=block(at, count),
                dst_ref=block(block_at(region, core, at_row), count),
                send_sem=fsend.at[which, number],
                recv_sem=frecv.at[which, region],
                device_id=(group, member),
                device_id_type=MESH,
            ).start()

    def wait_for(ref, sem):
        pltpu.make_async_copy(ref, ref, sem).wait()

    def landed(which, block, at_row):
        wait_for(block(block_at(1, core, at_row)), zrecv.at[which, at_row])

    def row_at(number):
        half = (number + 1) // 2
        return lax.rem(row + ROWS + lax.rem(number, 2) * 2 * half - half, ROWS)

    def pass_on(which, block):
        forward(which, block, row, 1)

        def close(number, carry):
            at_row = row_at(number)
            landed(which, block, at_row)
            send_row(which, block, at_row, ROWS + 4 - 8 * lax.rem(number, 2))
            forward(which, block, at_row, 1)
            return carry

        def rest(number, carry):
            at_row = row_at(number)
            landed(which, block, at_row)
            forward(which, block, at_row, 1)
            return carry

        lax.fori_loop(1, 7, close, 0)
        rest(jnp.int32(7), 0)
        at_row = lax.rem(row + ROWS - 4, ROWS)
        landed(which, block, at_row)
        send_row(which, block, at_row, 4)
        forward(which, block, at_row, 1)
        lax.fori_loop(9, ROWS, rest, 0)

    def pass_whole(which, block):
        def one(number, carry):
            landed(which, block, lax.rem(row + number, ROWS))
            return carry

        lax.fori_loop(1, ROWS, one, 0)
        forward(which, block, 0, ROWS)

    def arrived(which, block):
        wait_for(block(block_at(1, 0, 0), ROWS), frecv.at[which, 1])
        wait_for(block(block_at(0, 0, 0), 2 * ROWS), frecv.at[which, 0])
        wait_for(block(block_at(2, 0, 0), 2 * ROWS), frecv.at[which, 2])

    def all_sent(which, block):
        wait_for(block(0, ROWS - 1), zsend.at[which])
        for number in range(len(targets)):
            wait_for(block(0, ROWS), fsend.at[which, number])

    pl.semaphore_wait(barrier, len(near) + len(targets))
    for step in near:
        send_row(0, ext_block, row, step)
    for step in near:
        send_row(1, h_block, row, step)

    zero_row = jnp.zeros((1, LANES), jnp.float32)
    one_row = jnp.ones((1, LANES), jnp.float32)
    for cell in range(OWN):
        coords = [part[cell, axis : axis + 1, :] - 0.5 for axis in range(3)]
        highs = [high(value) for value in coords]
        lows = [high(value - top) for value, top in zip(coords, highs)]
        square = zero_row
        for top, low in zip(highs, lows):
            square = square + (top + low) * (top + low)
        part_a = high(square)
        part_b = high(square - part_a)
        part_c = square - part_a - part_b
        minus_high = [-2.0 * value for value in highs]
        minus_low = [-2.0 * value for value in lows]
        stacked = jnp.concatenate(
            minus_high + minus_high + [one_row] * 3 + [part_a, part_b, part_c] + [zero_row] * 4
            + minus_low + minus_low + [zero_row] * 10,
            axis=0,
        )
        wide = jnp.concatenate([stacked, jnp.zeros((LANES - 2 * FEAT, LANES), jnp.float32)], axis=0)
        left[cell] = wide.T[:, : 2 * FEAT].astype(jnp.bfloat16)
        invh[cell] = jnp.broadcast_to(2.0 / part[cell, 4:5, :], (LANES, LANES)).T

    def slot_cell(cell, number):
        ident = lists[cell, number]
        region = (lax.shift_right_logical(ident, GROUP_BITS) - grp + (GROUPS + 1)) & (GROUPS - 1)
        plane = lax.shift_left(ident & OWN, 4)
        at = region * GROUP_CELLS + plane + (lax.shift_right_logical(ident, 1) & 60) + (ident & (OWN - 1))
        live = jnp.minimum(jnp.maximum(counts[cell] - number, 0), 1)
        return CELLS + live * (at - CELLS)

    feat[pl.ds(CELLS * FEAT, FEAT), :] = jnp.zeros((FEAT, LANES), jnp.float32)
    mom[pl.ds(CELLS * 8, 8), :] = jnp.zeros((8, LANES), jnp.float32)
    wext[BLOCKS] = jnp.zeros((OWN, LANES), jnp.float32)
    ones = jnp.ones((8, LANES), jnp.float32)
    zeros = jnp.zeros((8, LANES), jnp.float32)

    def settle(number, carry):
        rows = number * 8 * FEAT
        for at in (9, 10, 11):
            feat[pl.ds(rows + at, 8, stride=FEAT), :] = ones
        for at in (13, 14, 15):
            feat[pl.ds(rows + at, 8, stride=FEAT), :] = zeros
        return carry

    lax.fori_loop(0, CELLS // 8, settle, 0)
    pass_on(0, ext_block)
    for step in far:
        send_row(1, h_block, row, step)
    arrived(0, ext_block)

    def planes(number):
        region = number // ROWS
        middle = 0.5 - (region - 1).astype(jnp.float32)

        def plane(axis):
            return ext[pl.ds(number * 32 + axis, 8, stride=4), :]

        return [plane(0) - middle, plane(1) - 0.5, plane(2) - 0.5], plane(3)

    def features(number, carry):
        coords, mass = planes(number)
        highs = [high(value) for value in coords]
        lows = [high(value - top) for value, top in zip(coords, highs)]
        square = zeros
        for top, low in zip(highs, lows):
            square = square + (top + low) * (top + low)
        part_a = high(square)
        part_b = high(square - part_a)
        part_c = square - part_a - part_b
        for at, value in enumerate(highs + lows + [part_a, part_b, part_c]):
            feat[pl.ds(number * 8 * FEAT + at, 8, stride=FEAT), :] = value
        feat[pl.ds(number * 8 * FEAT + 12, 8, stride=FEAT), :] = mass
        return carry

    lax.fori_loop(0, CELLS // 8, features, 0)

    def feature_rows(at):
        return feat[pl.ds(at * FEAT, FEAT), :]

    def density_cell(cell, carry):
        lhs = left[cell]
        scale = invh[cell]

        def step(turn, total):
            for pair in range(DENSITY_PAIRS):
                slot = (turn * DENSITY_PAIRS + pair) * 2
                rows = [feature_rows(slot_cell(cell, slot + which)) for which in range(2)]
                rhs = jnp.concatenate(rows, axis=1).astype(jnp.bfloat16)
                rhs = jnp.concatenate([rhs, rhs], axis=0)
                square = jnp.dot(lhs, rhs, preferred_element_type=jnp.float32)
                for which in range(2):
                    part_sq = jnp.maximum(square[:, which * LANES : (which + 1) * LANES], TINY)
                    gap = part_sq * lax.rsqrt(part_sq)
                    dist[cell * SLOTS + slot + which] = gap
                    base = jnp.maximum(4.0 - gap * scale, 0.0)
                    base_sq = base * base
                    total = total + base_sq * base_sq * (5.0 - base) * rows[which][12:13, :]
            return total

        total = lax.fori_loop(0, SLOTS // (2 * DENSITY_PAIRS), step, jnp.zeros((LANES, LANES), jnp.float32))
        summed = jnp.sum(total.T, axis=0, keepdims=True)
        smooth = part[cell, 4:5, :]
        density = summed * (NORM / 256.0) / (smooth * smooth * smooth)
        weight = entropy[pl.ds(cell, 1), :] * jnp.exp(jnp.log(density) * (-1.0 / 3.0))
        dens_out[pl.ds(cell, 1), :] = density
        wext[mine, pl.ds(cell, 1), :] = weight
        return carry

    lax.fori_loop(0, OWN, density_cell, 0)

    for step in far + near:
        send_row(2, w_block, row, step)

    pass_whole(1, h_block)

    def moments(number, carry):
        coords, mass = planes(number)
        values = [mass] + [mass * value for value in coords]
        for at, value in enumerate(values + values):
            mom[pl.ds(number * 64 + at, 8, stride=8), :] = value
        return carry

    lax.fori_loop(0, CELLS // 8, moments, 0)

    def smoothing(number, carry):
        smooth = jnp.concatenate([hext[2 * number], hext[2 * number + 1]], axis=0)
        inverse = 1.0 / smooth
        square = inverse * inverse
        feat[pl.ds(number * 8 * FEAT + 13, 8, stride=FEAT), :] = 2.0 * inverse
        feat[pl.ds(number * 8 * FEAT + 14, 8, stride=FEAT), :] = square * square * inverse
        return carry


    upper = lax.broadcasted_iota(jnp.int32, (8, LANES), 0) < 4

    def split(values):
        top = high(values)
        return jnp.where(upper, top, values - top).astype(jnp.bfloat16)

    def moment_rows(at):
        return mom[pl.ds(at * 8, 8), :]

    across = (((1,), (1,)), ((), ()))

    def first_cell(cell, carry):
        scale = invh[cell]

        def step(turn, total):
            tops, cubes = [], []
            for each in range(FIRST_SLOTS):
                slot = turn * FIRST_SLOTS + each
                at = slot_cell(cell, slot)
                tops.append(split(moment_rows(at)))
                gap = dist[cell * SLOTS + slot]
                base = jnp.maximum(4.0 - gap * scale, 0.0)
                cubes.append((base * base * base).astype(jnp.bfloat16))
            return total + lax.dot_general(
                jnp.concatenate(tops, axis=1), jnp.concatenate(cubes, axis=1), across,
                preferred_element_type=jnp.float32,
            )

        first[cell] = lax.fori_loop(0, SLOTS // FIRST_SLOTS, step, jnp.zeros((8, LANES), jnp.float32))
        return carry

    lax.fori_loop(0, OWN, first_cell, 0)
    arrived(1, h_block)
    lax.fori_loop(0, CELLS // 8, smoothing, 0)

    def cube_cell(cell, carry):
        def step(turn, inner):
            for each in range(FIRST_SLOTS):
                slot = turn * FIRST_SLOTS + each
                scale = feature_rows(slot_cell(cell, slot))[13:14, :]
                other = jnp.maximum(4.0 - dist[cell * SLOTS + slot] * scale, 0.0)
                cube[cell * SLOTS + slot] = (other * other * other).astype(jnp.bfloat16)
            return inner

        return lax.fori_loop(0, SLOTS // FIRST_SLOTS, step, carry)

    lax.fori_loop(0, OWN - 3, cube_cell, 0)
    pass_whole(2, w_block)
    lax.fori_loop(OWN - 3, OWN, cube_cell, 0)
    arrived(2, w_block)

    def force_cell(cell, carry):
        def step(turn, total):
            tops, cubes = [], []
            for each in range(FORCE_SLOTS):
                slot = turn * FORCE_SLOTS + each
                at = slot_cell(cell, slot)
                factor = wext[lax.shift_right_logical(at, 2), pl.ds(at & 3, 1), :] * feature_rows(at)[14:15, :]
                tops.append(split(moment_rows(at) * factor))
                cubes.append(cube[cell * SLOTS + slot])
            return total + lax.dot_general(
                jnp.concatenate(tops, axis=1), jnp.concatenate(cubes, axis=1), across,
                preferred_element_type=jnp.float32,
            )

        second = lax.fori_loop(0, SLOTS // FORCE_SLOTS, step, jnp.zeros((8, LANES), jnp.float32))
        second = second[0:4] + second[4:8]
        ahead = first[cell]
        ahead = ahead[0:4] + ahead[4:8]
        inverse = 1.0 / part[cell, 4:5, :]
        square = inverse * inverse
        own = wext[mine, pl.ds(cell, 1), :] * (square * square * inverse)
        joint = (own * ahead + second) * (5.0 * NORM / 64.0)
        coords = part[cell, 0:3, :] - 0.5
        acc_out[cell] = coords * joint[0:1] - joint[1:4]
        return carry

    lax.fori_loop(0, OWN, force_cell, 0)
    all_sent(0, ext_block)
    all_sent(1, h_block)
    all_sent(2, w_block)


def on_device(particles, entropy, lists, counts):
    vmem = pl.BlockSpec(memory_space=pltpu.VMEM)
    smem = pl.BlockSpec(memory_space=pltpu.SMEM)
    f32, bf16 = jnp.float32, jnp.bfloat16
    return pl.pallas_call(
        kernel,
        out_shape=(
            jax.ShapeDtypeStruct((OWN, LANES), f32),
            jax.ShapeDtypeStruct((OWN, 3, LANES), f32),
        ),
        in_specs=[smem, smem, vmem, vmem],
        out_specs=(vmem, vmem),
        scratch_shapes=[
            pltpu.VMEM((CELLS * 4, LANES), f32),
            pltpu.VMEM((BLOCKS, OWN, LANES), f32),
            pltpu.VMEM((BLOCKS + 1, OWN, LANES), f32),
            pltpu.VMEM(((CELLS + 1) * FEAT, LANES), f32),
            pltpu.VMEM(((CELLS + 1) * 8, LANES), f32),
            pltpu.VMEM((OWN, LANES, 2 * FEAT), bf16),
            pltpu.VMEM((OWN, LANES, LANES), f32),
            pltpu.VMEM((OWN * SLOTS, LANES, LANES), f32),
            pltpu.VMEM((OWN * SLOTS, LANES, LANES), bf16),
            pltpu.VMEM((OWN, 8, LANES), f32),
            pltpu.SemaphoreType.DMA((3,)),
            pltpu.SemaphoreType.DMA((3, ROWS)),
            pltpu.SemaphoreType.DMA((3, 5)),
            pltpu.SemaphoreType.DMA((3, 3)),
        ],
        compiler_params=pltpu.CompilerParams(
            collective_id=0, has_side_effects=True, vmem_limit_bytes=48 * 1024 * 1024
        ),
        name="sph",
    )(lists, counts, particles, entropy)


def solution(mesh):
    return jax.shard_map(
        on_device,
        mesh=mesh,
        in_specs=(
            P(("grp", "dev"), None, None),
            P(("grp", "dev"), None),
            P(("grp", "dev"), None),
            P(("grp", "dev")),
        ),
        out_specs=(P(("grp", "dev"), None), P(("grp", "dev"), None, None)),
        check_vma=False,
    )
```
